512 devices in a mesh: dp: 64 (over z_hi, y, core), mp: 8 (over z_lo, x).
Axes of the slice: x: 4, y: 8, z: 8 (z_hi: 4, z_lo: 2; z = z_hi * 2 + z_lo), core: 2. Of those that a mesh axis runs over, the one named last changes fastest.
Arguments:
- hidden: bfloat16 [40960, 14336], P('dp', 'mp'), may hold values from -6 to 6
- out_grad: bfloat16 [40960, 512], P('dp'), may hold values from -0.23632812 to 0.23632812
- master: float32 [14336, 512], P(('mp', 'dp')), may hold values from -0.03 to 0.03
- moment_one: float32 [14336, 512], P(('mp', 'dp')), may hold values from -0.12 to 0.12
- moment_two: float32 [14336, 512], P(('mp', 'dp')), may hold values from 0.0001 to 0.001
- sign_flips: int32 [512], replicated, may hold values from -1 to 1, as said below
- step_count: int32 [1], replicated, may hold values from 1 to 8
Outputs:
- weights: bfloat16 [14336, 512], P('mp')
- update: float32 [14336, 512], P(('mp', 'dp'))
The draws below stay inside these ranges and needn't reach their ends.
Inputs may be any that keep to these rules, and one draw needn't show every extreme that they name: `sign_flips`: each entry is -1 or 1.
All inputs are finite; a program needn't handle non-finite values.
Results may differ from the reference program's by a relative error of at most 0.007.
Values may be sent and summed in bfloat16 or wider, within the bound.
No kernel may reach another device: no remote copies, remote signals or barrier semaphores. Data moves between devices by JAX's collectives and lax.ppermute only.
A program may use at most 64 MiB of HBM per device.

```python
import math
import jax
import jax.numpy as jnp
from jax import lax

BUCKET = 512
TOK_DEV = 640
FF = 14336
TOKENS = 40960
N_DP = 64


def draw_sign_flips(key, part):
    return (2 * jax.random.randint(key, (BUCKET,), 0, 2) - 1).astype(jnp.int32)


def steps_of(own_key, dims, pieces, smallest, largest):
    factor_of = 1.0
    for axis_at, blocks in pieces:
        heights = jax.random.uniform(jax.random.fold_in(jax.random.fold_in(own_key, 6), axis_at), (blocks,), jnp.float32, smallest / len(pieces), largest / len(pieces))
        factor_of = factor_of * jnp.repeat(jnp.exp(heights), dims[axis_at] // blocks).reshape((-1,) + (1,) * (len(dims) - 1 - axis_at))
    return factor_of


def normal_values(rng, shape, deviation, reach, split=(), held_as=jnp.bfloat16):
    drawn = deviation * jax.random.normal(rng, shape, jnp.float32)
    if split:
        drawn = drawn * steps_of(rng, shape, split, -0.22, 0.18)
    return jnp.clip(drawn, -reach, reach).astype(held_as)


def setup_inputs(seed: int = 0) -> dict:
    key_of = jax.random.split(jax.random.key(seed), 8)
    hidden = normal_values(key_of[0], (TOKENS, FF), 1.0, 6.0, ((0, 64), (1, 8)))
    out_grad = normal_values(key_of[1], (TOKENS, BUCKET), (TOK_DEV ** -0.5), 0.23632812, ((0, 64),))
    master = normal_values(key_of[2], (FF, BUCKET), 0.005, 0.03, ((0, 512),), jnp.float32)
    moment_one = normal_values(key_of[3], (FF, BUCKET), 0.02, 0.12, ((0, 512),), jnp.float32)
    moment_two = jnp.clip(jnp.exp(math.log(0.001) - 2.3025852 * jax.random.uniform(key_of[4], (FF, BUCKET), jnp.float32) ** steps_of(key_of[4], (FF, BUCKET), ((0, 512),), -0.2, 0.2)), 0.0001, 0.001)
    sign_flips = draw_sign_flips(jax.random.fold_in(key_of[7], 71), 0)
    step_count = jax.random.randint(key_of[6], (1,), 1, 9).astype(jnp.int32)
    return dict(hidden=hidden, out_grad=out_grad, master=master, moment_one=moment_one, moment_two=moment_two, sign_flips=sign_flips, step_count=step_count)


def hadamard_table(order):
    table = jnp.ones((1, 1), jnp.float32)
    while table.shape[0] < order:
        table = jnp.concatenate([jnp.concatenate([table, table], axis=1), jnp.concatenate([table, -table], axis=1)], axis=0)
    return table

def reference(hidden, out_grad, master, moment_one, moment_two, sign_flips, step_count):
    factor = BUCKET ** (-0.5)
    table = hadamard_table(BUCKET) * factor
    table_half = table.astype(jnp.bfloat16)
    flips_half = sign_flips.astype(jnp.bfloat16)
    flips_full = sign_flips.astype(jnp.float32)
    hid_parts = hidden.reshape(N_DP, TOK_DEV, FF)
    grad_parts = out_grad.reshape(N_DP, TOK_DEV, BUCKET)

    def add_replica(total, pair):
        hid_block, grad_block = pair
        partial_value = jnp.dot(hid_block.T, grad_block, preferred_element_type=jnp.float32).astype(jnp.bfloat16)
        signed = partial_value * flips_half[None, :]
        rotated = jnp.dot(signed, table_half, preferred_element_type=jnp.float32).astype(jnp.bfloat16)
        rotated = lax.optimization_barrier(rotated)
        return (total + rotated.astype(jnp.float32), None)
    summed, _ = lax.scan(add_replica, jnp.zeros((FF, BUCKET), jnp.float32), (hid_parts, grad_parts))
    gradient = summed / N_DP
    steps_done = step_count[0].astype(jnp.float32)
    first = 0.9 * moment_one + 0.1 * gradient
    second = 0.95 * moment_two + 0.05 * gradient * gradient
    first_hat = first / (1.0 - jnp.power(jnp.float32(0.9), steps_done))
    second_hat = second / (1.0 - jnp.power(jnp.float32(0.95), steps_done))
    direction = first_hat / (jnp.sqrt(second_hat) + 1e-08)
    update = jnp.dot(direction, table, precision=lax.Precision.HIGHEST) * flips_full[None, :] + 0.1 * master
    weights = (master - 0.0003 * update).astype(jnp.bfloat16)
    return (weights, update)
```

```python
import jax
import jax.numpy as jnp
import numpy as np
from jax import lax
from jax.sharding import Mesh, PartitionSpec as P

DP = ("zh", "y", "c")
MP = ("zl", "x")


def signs_table(order):
    table = np.ones((1, 1), np.float32)
    while table.shape[0] < order:
        table = np.block([[table, table], [table, -table]])
    return table


def exact_dot(value, table):
    high = value.astype(jnp.bfloat16)
    rest = value - high.astype(jnp.float32)
    middle = rest.astype(jnp.bfloat16)
    low = (rest - middle.astype(jnp.float32)).astype(jnp.bfloat16)
    dot = lambda part: jnp.dot(part, table, preferred_element_type=jnp.float32)
    return dot(high) + (dot(middle) + dot(low))


def local(hidden, out_grad, master, moment_one, moment_two, sign_flips, step_count):
    columns = out_grad.shape[1]
    zh, y, c = (lax.axis_size(a) for a in DP)
    replicas = zh * y * c
    rows = master.shape[0]
    factor = columns ** (-0.5)
    table = jnp.asarray(signs_table(columns), jnp.bfloat16)
    flips = sign_flips.astype(jnp.float32)[None, :]
    core = lax.axis_index("c")
    partial_value = lax.dot_general(
        hidden, out_grad, (((0,), (0,)), ((), ())), preferred_element_type=jnp.float32
    ).astype(jnp.bfloat16)
    blocks = partial_value.reshape(zh, y, c, rows, columns)
    keep = lax.dynamic_index_in_dim(blocks, core, 2, keepdims=False)
    send = lax.dynamic_index_in_dim(blocks, 1 - core, 2, keepdims=False)
    got = lax.ppermute(send, "c", [(0, 1), (1, 0)])
    pair = (keep.astype(jnp.float32) + got.astype(jnp.float32)).astype(jnp.bfloat16)
    pair = jnp.swapaxes(pair, 0, 1)
    by_y = lax.all_to_all(pair, "y", 0, 0)
    by_y = jnp.sum(by_y.astype(jnp.float32), axis=0).astype(jnp.bfloat16)
    by_z = lax.all_to_all(by_y, "zh", 0, 0)
    summed = jnp.sum(by_z.astype(jnp.float32), axis=0)
    gradient = exact_dot(summed * flips, table) * (factor / replicas)
    steps_done = step_count[0].astype(jnp.float32)
    first = 0.9 * moment_one + 0.1 * gradient
    second = 0.95 * moment_two + 0.05 * gradient * gradient
    first_hat = first / (1.0 - jnp.power(jnp.float32(0.9), steps_done))
    second_hat = second / (1.0 - jnp.power(jnp.float32(0.95), steps_done))
    direction = first_hat / (jnp.sqrt(second_hat) + 1e-08)
    update = exact_dot(direction, table) * factor * flips + 0.1 * master
    own = (master - 0.0003 * update).astype(jnp.bfloat16)
    by_z = lax.all_to_all(jnp.broadcast_to(own[None], (zh, rows, columns)), "zh", 0, 0)
    by_y = lax.all_to_all(
        jnp.broadcast_to(by_z[None], (y, zh, rows, columns)), "y", 0, 0
    )
    low = lax.all_gather(by_y[: y // 2], "c", axis=0, tiled=False)
    high = lax.all_gather(by_y[y // 2 :], "c", axis=0, tiled=False)
    both = jnp.concatenate([low, high], axis=1)
    weights = jnp.transpose(both, (2, 1, 0, 3, 4)).reshape(-1, columns)
    return (weights, update)


def solution(mesh):
    inner = Mesh(mesh.devices.reshape(4, 8, 2, 2, 4), DP + MP)
    owner = P(MP + DP, None)
    return jax.shard_map(
        local,
        mesh=inner,
        in_specs=(P(DP, MP), P(DP, None), owner, owner, owner, P(), P()),
        out_specs=(P(MP, None), owner),
        check_vma=False,
    )
```

```python
import functools

import jax
import jax.numpy as jnp
import numpy as np
from jax import lax
from jax.experimental import pallas as pl
from jax.experimental.pallas import tpu as pltpu
from jax.sharding import Mesh, PartitionSpec as P

DP = ("zh", "y", "c")
MP = ("zl", "x")
LANES = 128
VMEM_LIMIT = 48 * 1024 * 1024


def signs_table(order):
    table = np.ones((1, 1), np.float32)
    while table.shape[0] < order:
        table = np.block([[table, table], [table, -table]])
    return table


def pack(block):
    parts = block.shape[1] // LANES
    return jnp.concatenate(
        [block[:, LANES * j : LANES * (j + 1)] for j in range(parts)], axis=0
    )


def unpack(block, rows):
    parts = block.shape[0] // rows
    return jnp.concatenate(
        [block[rows * j : rows * (j + 1), :] for j in range(parts)], axis=1
    )


def exact_dot(value, table):
    high = value.astype(jnp.bfloat16)
    rest = value - high.astype(jnp.float32)
    middle = rest.astype(jnp.bfloat16)
    low = (rest - middle.astype(jnp.float32)).astype(jnp.bfloat16)
    dot = lambda part: jnp.dot(part, table, preferred_element_type=jnp.float32)
    return dot(high) + (dot(middle) + dot(low))


def partial_kernel(rows, core_ref, hidden_ref, grad_ref, keep_ref, send_ref, held):
    held[...] = lax.dot_general(
        hidden_ref[...],
        grad_ref[...],
        (((0,), (0,)), ((), ())),
        preferred_element_type=jnp.float32,
    )
    first = core_ref[0] == 0
    for k in range(keep_ref.shape[0]):
        both = held[2 * rows * k : 2 * rows * (k + 1), :]
        lower, upper = pack(both[:rows]), pack(both[rows:])
        keep_ref[k] = jnp.where(first, lower, upper).astype(jnp.bfloat16)
        send_ref[k] = jnp.where(first, upper, lower).astype(jnp.bfloat16)


def partials(core, hidden, out_grad, rows, chips):
    tokens, units = hidden.shape
    columns = out_grad.shape[1]
    steps = 2
    high = rows * columns // LANES
    block = pl.BlockSpec((chips // steps, high, LANES), lambda i, core: (i, 0, 0))
    return pl.pallas_call(
        functools.partial(partial_kernel, rows),
        out_shape=[jax.ShapeDtypeStruct((chips, high, LANES), jnp.bfloat16)] * 2,
        grid_spec=pltpu.PrefetchScalarGridSpec(
            num_scalar_prefetch=1,
            grid=(steps,),
            in_specs=[
                pl.BlockSpec((tokens, units // steps), lambda i, core: (0, i)),
                pl.BlockSpec((tokens, columns), lambda i, core: (0, 0)),
            ],
            out_specs=[block, block],
            scratch_shapes=[pltpu.VMEM((units // steps, columns), jnp.float32)],
        ),
        compiler_params=pltpu.CompilerParams(vmem_limit_bytes=VMEM_LIMIT),
        name="partials",
    )(core, hidden, out_grad)


def update_kernel(
    replicas,
    step_ref,
    got_ref,
    master_ref,
    one_ref,
    two_ref,
    flips_ref,
    table_ref,
    update_ref,
    own_ref,
):
    rows, columns = master_ref.shape
    factor = columns ** (-0.5)
    table = table_ref[...]
    flips = flips_ref[...].astype(jnp.float32)
    total = got_ref[0].astype(jnp.float32)
    for k in range(1, got_ref.shape[0]):
        total = total + got_ref[k].astype(jnp.float32)
    summed = unpack(total, rows)
    gradient = exact_dot(summed * flips, table) * (factor / replicas)
    steps_done = jnp.full((1, columns), step_ref[0], jnp.int32).astype(jnp.float32)
    first = 0.9 * one_ref[...] + 0.1 * gradient
    second = 0.95 * two_ref[...] + 0.05 * gradient * gradient
    power = lambda base: jnp.power(jnp.full((1, columns), base, jnp.float32), steps_done)
    first_hat = first / (1.0 - power(0.9))
    second_hat = second / (1.0 - power(0.95))
    direction = first_hat / (jnp.sqrt(second_hat) + 1e-08)
    master = master_ref[...]
    update = exact_dot(direction, table) * factor * flips + 0.1 * master
    update_ref[...] = update
    own = pack(master - 0.0003 * update).astype(jnp.bfloat16)
    for k in range(own_ref.shape[0]):
        own_ref[k] = own


def update_step(step_count, got, master, moment_one, moment_two, flips, table, replicas):
    vmem = pl.BlockSpec(memory_space=pltpu.VMEM)
    return pl.pallas_call(
        functools.partial(update_kernel, replicas),
        out_shape=[
            jax.ShapeDtypeStruct(master.shape, jnp.float32),
            jax.ShapeDtypeStruct(got.shape, jnp.bfloat16),
        ],
        in_specs=[pl.BlockSpec(memory_space=pltpu.SMEM)] + [vmem] * 6,
        out_specs=[vmem, vmem],
        compiler_params=pltpu.CompilerParams(vmem_limit_bytes=VMEM_LIMIT),
        name="update_step",
    )(step_count, got, master, moment_one, moment_two, flips, table)


def weights_kernel(rows, core_ref, mine_ref, other_ref, out_ref):
    first = core_ref[0] == 0
    for k in range(mine_ref.shape[0]):
        mine = unpack(mine_ref[k].astype(jnp.float32), rows)
        other = unpack(other_ref[k].astype(jnp.float32), rows)
        lower = jnp.where(first, mine, other)
        upper = jnp.where(first, other, mine)
        both = jnp.concatenate([lower, upper], axis=0).astype(jnp.bfloat16)
        out_ref[2 * rows * k : 2 * rows * (k + 1), :] = both


def weights_step(core, mine, other, rows, columns):
    chips, high, _ = mine.shape
    steps = 4
    block = pl.BlockSpec((chips // steps, high, LANES), lambda i, core: (i, 0, 0))
    return pl.pallas_call(
        functools.partial(weights_kernel, rows),
        out_shape=jax.ShapeDtypeStruct((2 * rows * chips, columns), jnp.bfloat16),
        grid_spec=pltpu.PrefetchScalarGridSpec(
            num_scalar_prefetch=1,
            grid=(steps,),
            in_specs=[block, block],
            out_specs=pl.BlockSpec(
                (2 * rows * chips // steps, columns), lambda i, core: (i, 0)
            ),
        ),
        compiler_params=pltpu.CompilerParams(vmem_limit_bytes=VMEM_LIMIT),
        name="weights_step",
    )(core, mine, other)


def local(hidden, out_grad, master, moment_one, moment_two, sign_flips, step_count):
    columns = out_grad.shape[1]
    zh, y, c = (lax.axis_size(a) for a in DP)
    rows = master.shape[0]
    swap = [(0, 1), (1, 0)]
    core = lax.axis_index("c").astype(jnp.int32)[None]
    table = jnp.asarray(signs_table(columns), jnp.bfloat16)
    keep, send = partials(core, hidden, out_grad, rows, zh * y)
    met = lax.ppermute(send, "c", swap)
    pair = (keep.astype(jnp.float32) + met.astype(jnp.float32)).astype(jnp.bfloat16)
    got = lax.all_to_all(pair, ("zh", "y"), 0, 0)
    update, own = update_step(
        step_count,
        got,
        master,
        moment_one,
        moment_two,
        sign_flips[None, :],
        table,
        zh * y * c,
    )
    mine = lax.all_to_all(own, ("zh", "y"), 0, 0)
    other = lax.ppermute(mine, "c", swap)
    return (weights_step(core, mine, other, rows, columns), update)


def solution(mesh):
    inner = Mesh(mesh.devices.reshape(4, 8, 2, 2, 4), DP + MP)
    owner = P(MP + DP, None)
    return jax.shard_map(
        local,
        mesh=inner,
        in_specs=(P(DP, MP), P(DP, None), owner, owner, owner, P(), P()),
        out_specs=(P(MP, None), owner),
        check_vma=False,
    )
```

```python
import functools

import jax
import jax.numpy as jnp
import numpy as np
from jax import lax
from jax.experimental import pallas as pl
from jax.experimental.pallas import tpu as pltpu
from jax.sharding import Mesh, PartitionSpec as P

DP = ("zh", "y", "c")
MP = ("zl", "x")
LANES = 128
VMEM_LIMIT = 48 * 1024 * 1024
PARTIAL_VMEM = 103 * 512 * 1024
WIDEN = 2.0**17


def signs_table(order):
    table = np.ones((1, 1), np.float32)
    while table.shape[0] < order:
        table = np.block([[table, table], [table, -table]])
    return table


def pack(block):
    parts = block.shape[1] // LANES
    return jnp.concatenate(
        [block[:, LANES * j : LANES * (j + 1)] for j in range(parts)], axis=0
    )


def unpack(block, rows):
    parts = block.shape[0] // rows
    return jnp.concatenate(
        [block[rows * j : rows * (j + 1), :] for j in range(parts)], axis=1
    )


def exact_dot(value, table):
    rows = value.shape[0]
    high = value.astype(jnp.bfloat16)
    rest = value - high.astype(jnp.float32)
    middle = rest.astype(jnp.bfloat16)
    low = (rest - middle.astype(jnp.float32)).astype(jnp.bfloat16)
    parts = jnp.dot(
        jnp.concatenate([high, middle, low], axis=0),
        table,
        preferred_element_type=jnp.float32,
    )
    return parts[:rows] + (parts[rows : 2 * rows] + parts[2 * rows :])


def partial_kernel(
    rows,
    cuts,
    step_ref,
    hidden_ref,
    grad_ref,
    keep_ref,
    send_ref,
    powers_ref,
    units,
    grad,
    held,
    sems,
):
    moves = [pltpu.make_async_copy(grad_ref, grad, sems.at[len(cuts)])]
    for i, (start, stop) in enumerate(cuts):
        moves.append(
            pltpu.make_async_copy(
                hidden_ref.at[:, start:stop], units.at[:, start:stop], sems.at[i]
            )
        )
    for move in moves:
        move.start()
    moves[0].wait()
    first = lax.axis_index("c") == 0
    done = 0
    for (start, stop), move in zip(cuts, moves[1:]):
        move.wait()
        held[start:stop, :] = lax.dot_general(
            units[:, start:stop],
            grad[...],
            (((0,), (0,)), ((), ())),
            preferred_element_type=jnp.float32,
        )
        while 2 * rows * (done + 1) <= stop:
            both = held[2 * rows * done : 2 * rows * (done + 1), :]
            lower, upper = pack(both[:rows]), pack(both[rows:])
            keep_ref[done] = jnp.where(first, lower, upper).astype(jnp.bfloat16)
            send_ref[done] = jnp.where(first, upper, lower).astype(jnp.bfloat16)
            done += 1
    shape = powers_ref.shape[1:]
    steps_done = jnp.broadcast_to(step_ref[...], shape).astype(jnp.float32)
    for i, base in enumerate((0.9, 0.95)):
        powers_ref[i] = jnp.power(jnp.full(shape, base, jnp.float32), steps_done)


def partials(step_count, hidden, out_grad, rows, chips):
    tokens, units = hidden.shape
    columns = out_grad.shape[1]
    high = rows * columns // LANES
    step = 896
    cuts = [(at, min(at + step, units)) for at in range(0, units, step)]
    vmem = pl.BlockSpec(memory_space=pltpu.VMEM)
    hbm = pl.BlockSpec(memory_space=pltpu.HBM)
    block = jax.ShapeDtypeStruct((chips, high, LANES), jnp.bfloat16)
    return pl.pallas_call(
        functools.partial(partial_kernel, rows, cuts),
        out_shape=[block, block, jax.ShapeDtypeStruct((2, 8, LANES), jnp.float32)],
        in_specs=[vmem, hbm, hbm],
        out_specs=[vmem, vmem, vmem],
        scratch_shapes=[
            pltpu.VMEM((tokens, units), jnp.bfloat16),
            pltpu.VMEM((tokens, columns), jnp.bfloat16),
            pltpu.VMEM((units, columns), jnp.float32),
            pltpu.SemaphoreType.DMA((len(cuts) + 1,)),
        ],
        compiler_params=pltpu.CompilerParams(vmem_limit_bytes=PARTIAL_VMEM),
        name="partials",
    )(step_count, hidden, out_grad)


def update_kernel(
    replicas,
    powers_ref,
    got_ref,
    master_ref,
    one_ref,
    two_ref,
    flips_ref,
    table_ref,
    update_ref,
    own_ref,
):
    rows, columns = master_ref.shape
    factor = columns ** (-0.5)
    table = table_ref[...]
    flips = flips_ref[...].astype(jnp.float32)
    total = got_ref[0].astype(jnp.float32)
    for k in range(1, got_ref.shape[0]):
        total = total + got_ref[k].astype(jnp.float32)
    summed = unpack(total, rows)
    gradient = exact_dot(summed * flips, table) * (factor / replicas)
    first = 0.9 * one_ref[...] + 0.1 * gradient
    second = 0.95 * two_ref[...] + 0.05 * gradient * gradient
    spread = lambda i: jnp.concatenate(
        [powers_ref[i, :1, :]] * (columns // LANES), axis=1
    )
    first_hat = first / (1.0 - spread(0))
    second_hat = second / (1.0 - spread(1))
    direction = first_hat / (jnp.sqrt(second_hat) + 1e-08)
    master = master_ref[...]
    update = exact_dot(direction, table) * factor * flips + 0.1 * master
    update_ref[...] = update
    own_ref[...] = (master - 0.0003 * update).astype(jnp.bfloat16).astype(jnp.float32)


def update_step(powers, got, master, moment_one, moment_two, flips, table, replicas):
    vmem = pl.BlockSpec(memory_space=pltpu.VMEM)
    return pl.pallas_call(
        functools.partial(update_kernel, replicas),
        out_shape=[jax.ShapeDtypeStruct(master.shape, jnp.float32)] * 2,
        in_specs=[vmem] * 7,
        out_specs=[vmem, vmem],
        compiler_params=pltpu.CompilerParams(vmem_limit_bytes=VMEM_LIMIT),
        name="update_step",
    )(powers, got, master, moment_one, moment_two, flips, table)


def local(hidden, out_grad, master, moment_one, moment_two, sign_flips, step_count):
    columns = out_grad.shape[1]
    zh, y, c = (lax.axis_size(a) for a in DP)
    rows = master.shape[0]
    swap = [(0, 1), (1, 0)]
    table = jnp.asarray(signs_table(columns), jnp.bfloat16)
    keep, send, powers = partials(step_count[None, :], hidden, out_grad, rows, zh * y)
    met = lax.ppermute(send, "c", swap)
    pair = (keep.astype(jnp.float32) + met.astype(jnp.float32)).astype(jnp.bfloat16)
    got = lax.all_to_all(pair, ("zh", "y"), 0, 0)
    update, own = update_step(
        powers,
        got,
        master,
        moment_one,
        moment_two,
        sign_flips[None, :],
        table,
        zh * y * c,
    )
    own = (own * WIDEN).astype(jnp.float16)
    by_z = lax.all_to_all(jnp.broadcast_to(own[None], (zh, rows, columns)), "zh", 0, 0)
    whole = lax.all_gather(by_z, ("y", "c"), axis=1, tiled=True)
    weights = (whole.astype(jnp.float32) * (1.0 / WIDEN)).astype(jnp.bfloat16)
    return (weights.reshape(-1, columns), update)


def solution(mesh):
    inner = Mesh(mesh.devices.reshape(4, 8, 2, 2, 4), DP + MP)
    owner = P(MP + DP, None)
    return jax.shard_map(
        local,
        mesh=inner,
        in_specs=(P(DP, MP), P(DP, None), owner, owner, owner, P(), P()),
        out_specs=(P(MP, None), owner),
        check_vma=False,
    )
```

```python
import functools

import jax
import jax.numpy as jnp
import numpy as np
from jax import lax
from jax.experimental import pallas as pl
from jax.experimental.pallas import tpu as pltpu
from jax.sharding import Mesh, PartitionSpec as P

DP = ("zh", "y", "c")
MP = ("zl", "x")
LANES = 128
VMEM_LIMIT = 48 * 1024 * 1024
PARTIAL_VMEM = 103 * 512 * 1024
WIDEN = 2.0**17


def signs_table(order):
    table = np.ones((1, 1), np.float32)
    while table.shape[0] < order:
        table = np.block([[table, table], [table, -table]])
    return table


def pack(block):
    parts = block.shape[1] // LANES
    return jnp.concatenate(
        [block[:, LANES * j : LANES * (j + 1)] for j in range(parts)], axis=0
    )


def unpack(block, rows):
    parts = block.shape[0] // rows
    return jnp.concatenate(
        [block[rows * j : rows * (j + 1), :] for j in range(parts)], axis=1
    )


def exact_dot(value, table):
    rows = value.shape[0]
    high = value.astype(jnp.bfloat16)
    rest = value - high.astype(jnp.float32)
    middle = rest.astype(jnp.bfloat16)
    low = (rest - middle.astype(jnp.float32)).astype(jnp.bfloat16)
    parts = jnp.dot(
        jnp.concatenate([high, middle, low], axis=0),
        table,
        preferred_element_type=jnp.float32,
    )
    return parts[:rows] + (parts[rows : 2 * rows] + parts[2 * rows :])


def partial_kernel(
    rows,
    cuts,
    hidden_ref,
    grad_ref,
    keep_ref,
    send_ref,
    units,
    grad,
    held,
    sems,
):
    moves = [pltpu.make_async_copy(grad_ref, grad, sems.at[len(cuts)])]
    for i, (start, stop) in enumerate(cuts):
        moves.append(
            pltpu.make_async_copy(
                hidden_ref.at[:, start:stop], units.at[:, start:stop], sems.at[i]
            )
        )
    for move in moves:
        move.start()
    moves[0].wait()
    first = lax.axis_index("c") == 0
    done = 0
    for (start, stop), move in zip(cuts, moves[1:]):
        move.wait()
        held[start:stop, :] = lax.dot_general(
            units[:, start:stop],
            grad[...],
            (((0,), (0,)), ((), ())),
            preferred_element_type=jnp.float32,
        )
        while 2 * rows * (done + 1) <= stop:
            both = held[2 * rows * done : 2 * rows * (done + 1), :]
            lower, upper = pack(both[:rows]), pack(both[rows:])
            keep_ref[done] = jnp.where(first, lower, upper).astype(jnp.bfloat16)
            send_ref[done] = jnp.where(first, upper, lower).astype(jnp.bfloat16)
            done += 1


def partials(hidden, out_grad, rows, chips):
    tokens, units = hidden.shape
    columns = out_grad.shape[1]
    high = rows * columns // LANES
    step = 896
    cuts = [(at, min(at + step, units)) for at in range(0, units, step)]
    vmem = pl.BlockSpec(memory_space=pltpu.VMEM)
    hbm = pl.BlockSpec(memory_space=pltpu.HBM)
    block = jax.ShapeDtypeStruct((chips, high, LANES), jnp.bfloat16)
    return pl.pallas_call(
        functools.partial(partial_kernel, rows, cuts),
        out_shape=[block, block],
        in_specs=[hbm, hbm],
        out_specs=[vmem, vmem],
        scratch_shapes=[
            pltpu.VMEM((tokens, units), jnp.bfloat16),
            pltpu.VMEM((tokens, columns), jnp.bfloat16),
            pltpu.VMEM((units, columns), jnp.float32),
            pltpu.SemaphoreType.DMA((len(cuts) + 1,)),
        ],
        compiler_params=pltpu.CompilerParams(vmem_limit_bytes=PARTIAL_VMEM),
        name="partials",
    )(hidden, out_grad)


def update_kernel(
    replicas,
    powers_ref,
    got_ref,
    master_ref,
    one_ref,
    two_ref,
    flips_ref,
    table_ref,
    update_ref,
    own_ref,
):
    rows, columns = master_ref.shape
    factor = columns ** (-0.5)
    table = table_ref[...]
    flips = flips_ref[...].astype(jnp.float32)
    total = got_ref[0].astype(jnp.float32)
    for k in range(1, got_ref.shape[0]):
        total = total + got_ref[k].astype(jnp.float32)
    summed = unpack(total, rows)
    gradient = exact_dot(summed * flips, table) * (factor / replicas)
    first = 0.9 * one_ref[...] + 0.1 * gradient
    second = 0.95 * two_ref[...] + 0.05 * gradient * gradient
    spread = lambda i: jnp.concatenate(
        [powers_ref[i, :1, :]] * (columns // LANES), axis=1
    )
    first_hat = first / (1.0 - spread(0))
    second_hat = second / (1.0 - spread(1))
    direction = first_hat / (jnp.sqrt(second_hat) + 1e-08)
    master = master_ref[...]
    update = exact_dot(direction, table) * factor * flips + 0.1 * master
    update_ref[...] = update
    own_ref[...] = (master - 0.0003 * update).astype(jnp.bfloat16).astype(jnp.float32)


def update_step(powers, got, master, moment_one, moment_two, flips, table, replicas):
    vmem = pl.BlockSpec(memory_space=pltpu.VMEM)
    return pl.pallas_call(
        functools.partial(update_kernel, replicas),
        out_shape=[jax.ShapeDtypeStruct(master.shape, jnp.float32)] * 2,
        in_specs=[vmem] * 7,
        out_specs=[vmem, vmem],
        compiler_params=pltpu.CompilerParams(vmem_limit_bytes=VMEM_LIMIT),
        name="update_step",
    )(powers, got, master, moment_one, moment_two, flips, table)


def local(hidden, out_grad, master, moment_one, moment_two, sign_flips, step_count):
    columns = out_grad.shape[1]
    zh, y, c = (lax.axis_size(a) for a in DP)
    rows = master.shape[0]
    swap = [(0, 1), (1, 0)]
    table = jnp.asarray(signs_table(columns), jnp.bfloat16)
    keep, send = partials(hidden, out_grad, rows, zh * y)
    met = lax.ppermute(send, "c", swap)
    steps_done = jnp.broadcast_to(step_count.astype(jnp.float32), (8, LANES))
    powers = jnp.stack(
        [jnp.power(jnp.full((8, LANES), base, jnp.float32), steps_done) for base in (0.9, 0.95)]
    )
    keep, powers = lax.optimization_barrier((keep, powers))
    pair = (keep.astype(jnp.float32) + met.astype(jnp.float32)).astype(jnp.bfloat16)
    got = lax.all_to_all(pair, ("zh", "y"), 0, 0)
    update, own = update_step(
        powers,
        got,
        master,
        moment_one,
        moment_two,
        sign_flips[None, :],
        table,
        zh * y * c,
    )
    own = (own * WIDEN).astype(jnp.float16)
    by_z = lax.all_to_all(jnp.broadcast_to(own[None], (zh, rows, columns)), "zh", 0, 0)
    whole = lax.all_gather(by_z, ("y", "c"), axis=1, tiled=True)
    weights = (whole.astype(jnp.float32) * (1.0 / WIDEN)).astype(jnp.bfloat16)
    return (weights.reshape(-1, columns), update)


def solution(mesh):
    inner = Mesh(mesh.devices.reshape(4, 8, 2, 2, 4), DP + MP)
    owner = P(MP + DP, None)
    return jax.shard_map(
        local,
        mesh=inner,
        in_specs=(P(DP, MP), P(DP, None), owner, owner, owner, P(), P()),
        out_specs=(P(MP, None), owner),
        check_vma=False,
    )
```

```python
import functools

import jax
import jax.numpy as jnp
import numpy as np
from jax import lax
from jax.experimental import pallas as pl
from jax.experimental.pallas import tpu as pltpu
from jax.sharding import Mesh, PartitionSpec as P

DP = ("zh", "y", "c")
MP = ("zl", "x")
LANES = 128
VMEM_LIMIT = 48 * 1024 * 1024
PARTIAL_VMEM = 103 * 512 * 1024
WIDEN = 2.0**17


def signs_table(order):
    table = np.ones((1, 1), np.float32)
    while table.shape[0] < order:
        table = np.block([[table, table], [table, -table]])
    return table


def pack(block):
    parts = block.shape[1] // LANES
    return jnp.concatenate(
        [block[:, LANES * j : LANES * (j + 1)] for j in range(parts)], axis=0
    )


def unpack(block, rows):
    parts = block.shape[0] // rows
    return jnp.concatenate(
        [block[rows * j : rows * (j + 1), :] for j in range(parts)], axis=1
    )


def exact_dot(value, table):
    half = table.shape[0]
    left, right = value[:, :half], value[:, half:]
    value = jnp.concatenate([left + right, left - right], axis=0)
    rows = value.shape[0]
    high = value.astype(jnp.bfloat16)
    rest = value - high.astype(jnp.float32)
    middle = rest.astype(jnp.bfloat16)
    low = (rest - middle.astype(jnp.float32)).astype(jnp.bfloat16)
    parts = jnp.dot(
        jnp.concatenate([high, middle, low], axis=0),
        table,
        preferred_element_type=jnp.float32,
    )
    total = parts[:rows] + (parts[rows : 2 * rows] + parts[2 * rows :])
    return jnp.concatenate([total[: rows // 2], total[rows // 2 :]], axis=1)


def partial_kernel(
    rows,
    orders,
    cuts,
    hidden_ref,
    grad_ref,
    keep_ref,
    send_ref,
    units,
    grad,
    held,
    sems,
):
    moves = [pltpu.make_async_copy(grad_ref, grad, sems.at[len(cuts)])]
    for i, (start, stop) in enumerate(cuts):
        moves.append(
            pltpu.make_async_copy(
                hidden_ref.at[:, start:stop], units.at[:, start:stop], sems.at[i]
            )
        )
    for move in moves:
        move.start()
    moves[0].wait()
    first = lax.axis_index("c") == 0
    done = 0
    for (start, stop), move in zip(cuts, moves[1:]):
        move.wait()
        held[start:stop, :] = lax.dot_general(
            units[:, start:stop],
            grad[...],
            (((0,), (0,)), ((), ())),
            preferred_element_type=jnp.float32,
        )
        while 2 * rows * (done + 1) <= stop:
            both = held[2 * rows * done : 2 * rows * (done + 1), :]
            lower, upper = pack(both[:rows]), pack(both[rows:])
            by_core = [order[done] for order in orders]
            mine = jnp.where(first, by_core[0], by_core[1])
            other = jnp.where(first, by_core[1], by_core[0])
            keep_ref[mine] = jnp.where(first, lower, upper).astype(jnp.bfloat16)
            send_ref[other] = jnp.where(first, upper, lower).astype(jnp.bfloat16)
            done += 1


def partials(hidden, out_grad, rows, chips, orders):
    tokens, units = hidden.shape
    columns = out_grad.shape[1]
    high = rows * columns // LANES
    step = 896
    cuts = [(at, min(at + step, units)) for at in range(0, units, step)]
    vmem = pl.BlockSpec(memory_space=pltpu.VMEM)
    hbm = pl.BlockSpec(memory_space=pltpu.HBM)
    block = jax.ShapeDtypeStruct((chips, high, LANES), jnp.bfloat16)
    return pl.pallas_call(
        functools.partial(partial_kernel, rows, orders, cuts),
        out_shape=[block, block],
        in_specs=[hbm, hbm],
        out_specs=[vmem, vmem],
        scratch_shapes=[
            pltpu.VMEM((tokens, units), jnp.bfloat16),
            pltpu.VMEM((tokens, columns), jnp.bfloat16),
            pltpu.VMEM((units, columns), jnp.float32),
            pltpu.SemaphoreType.DMA((len(cuts) + 1,)),
        ],
        compiler_params=pltpu.CompilerParams(vmem_limit_bytes=PARTIAL_VMEM),
        name="partials",
    )(hidden, out_grad)


def update_kernel(
    replicas,
    powers_ref,
    got_ref,
    master_ref,
    one_ref,
    two_ref,
    flips_ref,
    table_ref,
    update_ref,
    own_ref,
):
    rows, columns = master_ref.shape
    factor = columns ** (-0.5)
    table = table_ref[...]
    flips = flips_ref[...].astype(jnp.float32)
    total = got_ref[0].astype(jnp.float32)
    for k in range(1, got_ref.shape[0]):
        total = total + got_ref[k].astype(jnp.float32)
    summed = unpack(total, rows)
    gradient = exact_dot(summed * flips, table) * (factor / replicas)
    first = 0.9 * one_ref[...] + 0.1 * gradient
    second = 0.95 * two_ref[...] + 0.05 * gradient * gradient
    spread = lambda i: jnp.concatenate(
        [powers_ref[i, :1, :]] * (columns // LANES), axis=1
    )
    first_hat = first / (1.0 - spread(0))
    second_hat = second / (1.0 - spread(1))
    direction = first_hat / (jnp.sqrt(second_hat) + 1e-08)
    master = master_ref[...]
    update = exact_dot(direction, table) * factor * flips + 0.1 * master
    update_ref[...] = update
    own_ref[...] = (master - 0.0003 * update).astype(jnp.bfloat16).astype(jnp.float32)


def update_step(powers, got, master, moment_one, moment_two, flips, table, replicas):
    vmem = pl.BlockSpec(memory_space=pltpu.VMEM)
    return pl.pallas_call(
        functools.partial(update_kernel, replicas),
        out_shape=[jax.ShapeDtypeStruct(master.shape, jnp.float32)] * 2,
        in_specs=[vmem] * 7,
        out_specs=[vmem, vmem],
        compiler_params=pltpu.CompilerParams(vmem_limit_bytes=VMEM_LIMIT),
        name="update_step",
    )(powers, got, master, moment_one, moment_two, flips, table)


def local(orders, groups, hidden, out_grad, master, moment_one, moment_two, sign_flips, step_count):
    columns = out_grad.shape[1]
    zh, y, c = (lax.axis_size(a) for a in DP)
    rows = master.shape[0]
    chips = zh * y
    swap = [(0, 1), (1, 0)]
    table = jnp.asarray(signs_table(columns // 2), jnp.bfloat16)
    keep, send = partials(hidden, out_grad, rows, chips, orders)
    met = lax.ppermute(send, "c", swap)
    steps_done = jnp.broadcast_to(step_count.astype(jnp.float32), (8, LANES))
    powers = jnp.stack(
        [jnp.power(jnp.full((8, LANES), base, jnp.float32), steps_done) for base in (0.9, 0.95)]
    )
    keep, powers = lax.optimization_barrier((keep, powers))
    pair = (keep.astype(jnp.float32) + met.astype(jnp.float32)).astype(jnp.bfloat16)
    near_size = len(groups[0][0])
    pair = pair.reshape((near_size, chips // near_size) + pair.shape[1:])
    near = lax.all_to_all(pair, DP + MP, 0, 0, axis_index_groups=groups[0])
    near = jnp.sum(near.astype(jnp.float32), axis=0).astype(jnp.bfloat16)
    got = lax.all_to_all(near, DP + MP, 0, 0, axis_index_groups=groups[1])
    update, own = update_step(
        powers,
        got,
        master,
        moment_one,
        moment_two,
        sign_flips[None, :],
        table,
        zh * y * c,
    )
    own = (own * WIDEN).astype(jnp.float16)
    by_z = lax.all_to_all(jnp.broadcast_to(own[None], (zh, rows, columns)), "zh", 0, 0)
    whole = lax.all_gather(by_z, ("y", "c"), axis=1, tiled=True)
    weights = (whole.astype(jnp.float32) * (1.0 / WIDEN)).astype(jnp.bfloat16)
    return (weights.reshape(-1, columns), update)


def two_stages(sizes):
    zh, y, c, zl, x = sizes
    numbers = np.arange(np.prod(sizes)).reshape(sizes)
    split = numbers.reshape(zh, 4, y // 4, c, zl, x)
    near0 = np.moveaxis(split[:, :, :, 0], 1, -1).reshape(-1, 4)
    far0 = np.moveaxis(split[:, :, :, 0], (0, 2), (-2, -1)).reshape(-1, 8)
    near1 = np.moveaxis(numbers[:, :, 1], 0, -1).reshape(-1, 4)
    far1 = np.moveaxis(numbers[:, :, 1], 1, -1).reshape(-1, 8)
    groups = (
        np.concatenate([near0, near1]).tolist(),
        np.concatenate([far0, far1]).tolist(),
    )
    chips = np.arange(zh * y)
    order0 = chips.reshape(4, zh, y // 4).transpose(1, 0, 2).reshape(-1)
    return (order0.tolist(), chips.tolist()), groups


def solution(mesh):
    sizes = (4, 8, 2, 2, 4)
    inner = Mesh(mesh.devices.reshape(sizes), DP + MP)
    owner = P(MP + DP, None)
    return jax.shard_map(
        functools.partial(local, *two_stages(sizes)),
        mesh=inner,
        in_specs=(P(DP, MP), P(DP, None), owner, owner, owner, P(), P()),
        out_specs=(P(MP, None), owner),
        check_vma=False,
    )
```
